32 devices in a mesh: view: 4 (over y, x), gz: 8 (over z, core).
Axes of the slice: x: 2, y: 2, z: 4, core: 2. Of those that a mesh axis runs over, the one named last changes fastest.
Arguments:
- views_data: float32 [4, 128, 96, 1024], P('view', 'gz'), may hold values from 0.2 to 40
- estimate: float32 [128, 96, 1024], P('gz'), may hold values from 0.5 to 1.5
- kernels: float32 [4, 3, 31], P('view'), may hold values from 0.001 to 3
Outputs:
- deconvolved: float32 [128, 96, 1024], P('gz')
The draws below stay inside these ranges and needn't reach their ends.
All inputs are finite; a program needn't handle non-finite values.
Results may differ from the reference program's by a relative error of at most 0.0001.
Values sent between devices are 32-bit elements; how exact they have to be, the bound alone decides.
A program may use at most 128 MiB of HBM per device.

```python
import jax
import jax.numpy as jnp
from jax import lax

X = 1024
Y = 96
TAPS = 31
ITERS = 2
RADIUS = 15
VIEWS = 4
Z = 128


def draw_kernels(key, part):
    streams = jax.random.split(key, 5)
    offsets = (jnp.arange(TAPS) - RADIUS).astype(jnp.float32)
    lateral_sigma = jax.random.uniform(streams[0], (VIEWS, 2, 1), jnp.float32, 1.0, 2.0)
    lateral_scaled = offsets / lateral_sigma
    lateral = jnp.exp(-0.5 * lateral_scaled * lateral_scaled) + 0.002
    axial_sigma = jax.random.uniform(streams[1], (VIEWS, 1, 1), jnp.float32, 2.0, 4.0)
    axial_width = jax.random.uniform(streams[2], (VIEWS, 1, 1), jnp.float32, 3.0, 6.0)
    axial_weight = jax.random.uniform(streams[3], (VIEWS, 1, 1), jnp.float32, 0.3, 1.0)
    core_scaled = offsets / axial_sigma
    tail_scaled = offsets / axial_width
    axial = jnp.exp(-0.5 * core_scaled * core_scaled) + axial_weight / (1.0 + tail_scaled * tail_scaled)
    jitter = jax.random.uniform(streams[4], (VIEWS, 3, TAPS), jnp.float32, 0.8, 1.2)
    return jnp.concatenate([lateral, axial], axis=1) * jitter


def draw_views_data(key, part):
    streams = jax.random.split(key, 5)
    points = (jax.random.randint(streams[0], (Z, Y, X), 0, 16) == 0).astype(jnp.float32)
    bright = jax.random.uniform(streams[1], (Z, Y, X), jnp.float32, 2.0, 8.0)
    sample = 1.0 + points * bright
    loudness = jax.random.uniform(streams[3], (VIEWS, 1, 1, 1), jnp.float32, 0.6, 1.6)
    jitter = jax.random.uniform(streams[4], (VIEWS, Z, Y, X), jnp.float32, 0.75, 1.25)
    return loudness * sample[None] * jitter


def steps_of(rng, extent, cuts, smallest, largest):
    factor_of = 1.0
    for position, parts in cuts:
        steps = jax.random.uniform(jax.random.fold_in(jax.random.fold_in(rng, 6), position), (parts,), jnp.float32, smallest / len(cuts), largest / len(cuts))
        factor_of = factor_of * jnp.repeat(jnp.exp(steps), extent[position] // parts).reshape((-1,) + (1,) * (len(extent) - 1 - position))
    return factor_of


def setup_inputs(seed: int = 0) -> dict:
    arg_keys = jax.random.split(jax.random.key(seed), 4)
    views_data = draw_views_data(jax.random.fold_in(arg_keys[3], 71), 0)
    estimate = jnp.clip(0.5 + 1.0 * jax.random.uniform(arg_keys[1], (Z, Y, X), jnp.float32) ** steps_of(arg_keys[1], (Z, Y, X), ((0, 8),), -0.2, 0.2), 0.5, 1.5)
    kernels = draw_kernels(jax.random.fold_in(arg_keys[3], 71), 0)
    return dict(views_data=views_data, estimate=estimate, kernels=kernels)


def toeplitz(tap_values, count):
    row_pos = jnp.arange(count)[:, None]
    col_pos = jnp.arange(count)[None, :]
    offsets = row_pos - col_pos + RADIUS
    matrix = jnp.zeros((count, count), jnp.float32)
    for offset in range(TAPS):
        matrix = matrix + jnp.where(offsets == offset, tap_values[offset], 0.0)
    return matrix


def z_filter(volume, tap_values, flipped):
    depth = volume.shape[0]
    padded = jnp.pad(volume, ((RADIUS, RADIUS), (0, 0), (0, 0)))
    result = jnp.zeros_like(volume)
    for offset in range(TAPS):
        start = 2 * RADIUS - offset if flipped else offset
        result = result + tap_values[offset] * padded[start:start + depth]
    return result


def blur(volume, kernel_set, flipped):
    mat_x = toeplitz(kernel_set[0], volume.shape[2])
    mat_y = toeplitz(kernel_set[1], volume.shape[1])
    if flipped:
        mat_x = mat_x.T
        mat_y = mat_y.T
    passed = jnp.dot(volume, mat_x, precision=lax.Precision.HIGHEST)
    passed = jnp.einsum("zyx,yw->zwx", passed, mat_y, precision=lax.Precision.HIGHEST)
    return z_filter(passed, kernel_set[2], flipped)


def reference(views_data, estimate, kernels):
    tap_norm = kernels / jnp.sum(kernels, axis=-1, keepdims=True)
    for number in range(ITERS):
        logsum = jnp.zeros_like(estimate)
        for view_number in range(VIEWS):
            blurred = blur(estimate, tap_norm[view_number], False)
            ratio = views_data[view_number] / blurred
            back = blur(ratio, tap_norm[view_number], True)
            logsum = logsum + jnp.log(back)
        estimate = estimate * jnp.exp(logsum / VIEWS)
    return estimate
```

```python
import functools

import jax
import jax.numpy as jnp
from jax import lax
from jax.experimental import pallas as pl
from jax.experimental.pallas import tpu as pltpu
from jax.sharding import PartitionSpec as P

TAPS = 31
ITERS = 2
RADIUS = 15
LANES = 128
HALF = 64
VMEM_LIMIT = 40 * 1024 * 1024


def gray(p):
    return p ^ (p >> 1)


def ungray(g):
    g = g ^ (g >> 1)
    g = g ^ (g >> 2)
    return g ^ (g >> 4)


def split(value):
    hi = value.astype(jnp.bfloat16)
    lo = (value - hi.astype(jnp.float32)).astype(jnp.bfloat16)
    return hi, lo


def dot(a, b):
    return jnp.dot(a, b, preferred_element_type=jnp.float32)


def position(lane, width):
    return jnp.where(lane < width + HALF, lane, lane - width - LANES)


def matrices_kernel(width, taps, *refs):
    for view in range(taps.shape[0]):
        view_matrices(width, view, taps, *refs[6 * view : 6 * view + 6])


def view_matrices(width, view, taps, yf, ya, xfh, xfl, xah, xal):
    ylen = yf.shape[0] // 2
    full = width + LANES

    def banded(diff, axis):
        acc = jnp.zeros(diff.shape, jnp.float32)
        for t in range(TAPS):
            acc = jnp.where(diff == t, taps[view, axis, t], acc)
        return acc

    def rows(shape, start):
        return lax.broadcasted_iota(jnp.int32, shape, 0) + start

    def cols(shape):
        return lax.broadcasted_iota(jnp.int32, shape, 1)

    for s in range(0, ylen, 32):
        diff = cols((32, ylen)) - rows((32, ylen), s)
        for ref, d in ((yf, diff), (ya, -diff)):
            hi, lo = split(banded(d + RADIUS, 1))
            ref[s : s + 32, :] = jnp.concatenate([hi, hi], axis=1)
            ref[ylen + s : ylen + s + 32, :] = jnp.concatenate([lo, jnp.zeros_like(lo)], axis=1)

    def chunk(i, carry):
        s = pl.multiple_of(i * 32, 32)
        for o in range(0, full, LANES):
            shape = (32, LANES)
            diff = position(rows(shape, s), width) - position(cols(shape) + o, width)
            if o < width:
                hi, lo = split(banded(diff + RADIUS, 0))
                xfh[pl.ds(s, 32), o : o + LANES] = hi
                xfl[pl.ds(s, 32), o : o + LANES] = lo
            hi, lo = split(banded(RADIUS - diff, 0))
            xah[pl.ds(s, 32), o : o + LANES] = hi
            xal[pl.ds(s, 32), o : o + LANES] = lo
        return carry

    lax.fori_loop(0, full // 32, chunk, 0)


def z_pass(view, flipped, taps, low, own, high, out):
    depth, ylen, width = own.shape
    tiles = width // LANES
    t_of = [taps[view, 2, TAPS - 1 - t if flipped else t] for t in range(TAPS)]

    def body(i, carry):
        y = pl.ds(pl.multiple_of((i // tiles) * 8, 8), 8)
        x = pl.ds(pl.multiple_of((i % tiles) * LANES, LANES), LANES)
        acc = [None] * depth
        for p in range(depth + 2 * RADIUS):
            if p < RADIUS:
                plane = low[p, y, x]
            elif p < RADIUS + depth:
                plane = own[p - RADIUS, y, x]
            else:
                plane = high[p - RADIUS - depth, y, x]
            for o in range(depth):
                if 0 <= p - o < TAPS:
                    term = t_of[p - o] * plane
                    acc[o] = term if acc[o] is None else acc[o] + term
        for o in range(depth):
            out[o, y, x] = acc[o]
        return carry

    lax.fori_loop(0, (ylen // 8) * tiles, body, 0)


def y_pass(mat, plane):
    ylen = plane.shape[0]
    hi, lo = split(plane)
    both = dot(mat, jnp.concatenate([hi, lo], axis=0))
    return both[:ylen] + both[ylen:]


def x_pass(hi, lo, mat_hi, mat_lo):
    return dot(hi, mat_hi) + (dot(lo, mat_hi) + dot(hi, mat_lo))


def forward_kernel(view, divide, taps, low, own, high, yf, xfh, xfl, *refs):
    data = refs[0] if divide else None
    ratio, zed, hi_s, lo_s = refs[-4:]
    depth, ylen, _ = own.shape
    z_pass(view, False, taps, low, own, high, zed)
    mat = yf[...]
    for p in range(depth):
        hi, lo = split(y_pass(mat, zed[p]))
        hi_s[p * ylen : (p + 1) * ylen, :] = hi
        lo_s[p * ylen : (p + 1) * ylen, :] = lo
    for p in range(0, depth, 4):
        r = slice(p * ylen, (p + 4) * ylen)
        blurred = x_pass(hi_s[r, :], lo_s[r, :], xfh[...], xfl[...])
        blurred = blurred.reshape(4, ylen, -1)
        ratio[p : p + 4] = data[p : p + 4] / blurred if divide else blurred


def adjoint_zy_kernel(view, taps, low, own, high, ya, out, to_left, to_right, zed):
    depth, ylen, width = own.shape
    z_pass(view, True, taps, low, own, high, zed)
    mat = ya[...]
    for p in range(depth):
        out[p] = y_pass(mat, zed[p])
    lane = lax.broadcasted_iota(jnp.int32, (ylen, LANES), 1)
    half = depth // 2
    for p in range(half):
        first, first_b = out[p, :, :LANES], out[p + half, :, :LANES]
        last, last_b = out[p, :, width - LANES :], out[p + half, :, width - LANES :]
        to_left[p] = jnp.where(lane < HALF, first, pltpu.roll(first_b, HALF, 1))
        to_right[p] = jnp.where(lane < HALF, pltpu.roll(last_b, HALF, 1), last)


def adjoint_x_kernel(first, final, views, *refs):
    refs = list(refs)
    total = None if first else refs.pop(0)
    estimate = refs.pop(0) if final else None
    own, from_left, from_right, xah, xal, out, hi_s, lo_s = refs
    depth, ylen, width = own.shape
    cols = out.shape[2]
    half = depth // 2
    lane = lax.broadcasted_iota(jnp.int32, (ylen, LANES), 1)
    for p in range(depth):
        r = slice(p * ylen, (p + 1) * ylen)
        hi_s[r, :width], lo_s[r, :width] = split(own[p])
        q = p % half
        if p < half:
            halo = jnp.where(lane < HALF, from_right[q], from_left[q])
        else:
            halo = pltpu.roll(jnp.where(lane < HALF, from_left[q], from_right[q]), HALF, 1)
        hi_s[r, width:], lo_s[r, width:] = split(halo)
    for p in range(0, depth, 4):
        r = slice(p * ylen, (p + 4) * ylen)
        back = x_pass(hi_s[r, :], lo_s[r, :], xah[:, :cols], xal[:, :cols])
        logs = jnp.log(back.reshape(4, ylen, cols))
        if not first:
            logs = total[p : p + 4, :, :cols] + logs
        if final:
            logs = estimate[p : p + 4, :, :cols] * jnp.exp(logs / views)
        out[p : p + 4] = logs


def call(kernel, outs, ins, scratch, flops, moved):
    vmem = pl.BlockSpec(memory_space=pltpu.VMEM)
    return pl.pallas_call(
        kernel,
        out_shape=outs,
        in_specs=[spec if spec is not None else vmem for spec, _ in ins],
        out_specs=jax.tree.map(lambda _: vmem, outs),
        scratch_shapes=scratch,
        compiler_params=pltpu.CompilerParams(vmem_limit_bytes=VMEM_LIMIT),
        cost_estimate=pl.CostEstimate(flops=flops, bytes_accessed=moved, transcendentals=0),
    )(*[value for _, value in ins])


def per_device(views_data, estimate, kernels):
    f32, bf16 = jnp.float32, jnp.bfloat16
    depth, ylen, xlen = estimate.shape
    count = lax.axis_size("view")
    slabs = lax.axis_size("gz")
    width = xlen // count
    full = width + LANES
    me = lax.axis_index("view")
    place = ungray(me)

    def swap(value, k):
        if k == 0:
            return value
        return lax.ppermute(value, "view", [(d, d ^ k) for d in range(count)])

    up = [(i, i + 1) for i in range(slabs - 1)]
    down = [(i + 1, i) for i in range(slabs - 1)]
    rightward = [(gray(p), gray(p + 1)) for p in range(count - 1)]
    leftward = [(gray(p + 1), gray(p)) for p in range(count - 1)]

    def z_halo(value):
        low = lax.ppermute(value[depth - RADIUS :], "gz", up)
        high = lax.ppermute(value[:RADIUS], "gz", down)
        return low, high

    def columns(value, start, size):
        return lax.dynamic_slice_in_dim(value, start, size, axis=2)

    padded = jnp.pad(estimate, ((0, 0), (0, 0), (LANES, LANES)))
    own = columns(padded, place * width + LANES, width)
    right = columns(padded, place * width + LANES + width, LANES)[:, :, :HALF]
    left = columns(padded, place * width, LANES)[:, :, HALF:]
    est = jnp.concatenate([own, right, left], axis=2)
    halo = z_halo(est)

    norm = kernels[0] / jnp.sum(kernels[0], axis=-1, keepdims=True)

    def in_order(parts):
        return [lax.dynamic_index_in_dim(parts, me ^ v, 0, keepdims=False) for v in range(count)]

    taps = jnp.stack(in_order(jnp.stack([swap(norm, k) for k in range(count)])))
    data = [swap(columns(views_data[0], ungray(me ^ k) * width, width), k) for k in range(count)]
    data = in_order(jnp.stack(data))

    smem = pl.BlockSpec(memory_space=pltpu.SMEM)
    shapes = [(2 * ylen, 2 * ylen)] * 2 + [(full, width)] * 2 + [(full, full)] * 2
    mats = call(
        functools.partial(matrices_kernel, width),
        [jax.ShapeDtypeStruct(s, bf16) for _ in range(count) for s in shapes],
        [(smem, taps)],
        [],
        1000000,
        1000000,
    )
    yf, ya, xfh, xfl, xah, xal = [mats[i::6] for i in range(6)]

    slab = jax.ShapeDtypeStruct((depth, ylen, width), f32)
    wide = jax.ShapeDtypeStruct((depth, ylen, full), f32)
    edge = jax.ShapeDtypeStruct((depth // 2, ylen, LANES), f32)
    rows = depth * ylen
    halves = [pltpu.VMEM((rows, full), bf16)] * 2
    work = 2 * rows * full

    for number in range(ITERS):
        last = number == ITERS - 1
        ratios, halos = [], []
        for k in range(count):
            divide = number > 0
            ratio = call(
                functools.partial(forward_kernel, k, divide),
                slab,
                [(smem, taps), (None, halo[0]), (None, est), (None, halo[1])]
                + [(None, m[k]) for m in (yf, xfh, xfl)]
                + ([(None, data[k])] if divide else []),
                [pltpu.VMEM((depth, ylen, full), f32)] + halves,
                work * 3000,
                rows * full * 16,
            )
            if not divide:
                ratio = data[k] / ratio
            ratios.append(ratio)
            halos.append(z_halo(ratio))
        total = None
        for k in range(count):
            low, high = halos[k]
            back, to_left, to_right = call(
                functools.partial(adjoint_zy_kernel, k),
                [slab, edge, edge],
                [(smem, taps), (None, low), (None, ratios[k]), (None, high), (None, ya[k])],
                [pltpu.VMEM((depth, ylen, width), f32)],
                work * 2000,
                rows * full * 16,
            )
            from_right = lax.ppermute(to_left, "view", leftward)
            from_left = lax.ppermute(to_right, "view", rightward)
            final = k == count - 1
            ins = [] if total is None else [(None, total)]
            ins += [(None, est)] if final else []
            ins += [(None, back), (None, from_left), (None, from_right)]
            ins += [(None, m[k]) for m in (xah, xal)]
            total = call(
                functools.partial(adjoint_x_kernel, total is None, final, count),
                slab if last else wide,
                ins,
                halves,
                work * 2000,
                rows * full * 16,
            )
        est = total
        if not last:
            halo = z_halo(est)

    blocks = lax.all_gather(est, "view")
    return jnp.concatenate([blocks[gray(p)] for p in range(count)], axis=2)


def solution(mesh):
    return jax.shard_map(
        per_device,
        mesh=mesh,
        in_specs=(P("view", "gz", None, None), P("gz", None, None), P("view", None, None)),
        out_specs=P("gz", None, None),
        check_vma=False,
    )
```

```python
import functools

import jax
import jax.numpy as jnp
from jax import lax
from jax.experimental import pallas as pl
from jax.experimental.pallas import tpu as pltpu
from jax.sharding import PartitionSpec as P

TAPS = 31
ITERS = 2
RADIUS = 15
LANES = 128
HALF = 64
VMEM_LIMIT = 40 * 1024 * 1024


def gray(p):
    return p ^ (p >> 1)


def ungray(g):
    g = g ^ (g >> 1)
    g = g ^ (g >> 2)
    return g ^ (g >> 4)


def split(value):
    hi = value.astype(jnp.bfloat16)
    lo = (value - hi.astype(jnp.float32)).astype(jnp.bfloat16)
    return hi, lo


def dot(a, b):
    return jnp.dot(a, b, preferred_element_type=jnp.float32)


def position(lane, width):
    return jnp.where(lane < width + HALF, lane, lane - width - LANES)


def matrices_kernel(width, taps, *refs):
    for view in range(taps.shape[0]):
        view_matrices(width, view, taps, *refs[6 * view : 6 * view + 6])


def view_matrices(width, view, taps, yf, ya, xfh, xfl, xah, xal):
    ylen = yf.shape[0] // 2
    full = width + LANES

    def banded(diff, axis):
        acc = jnp.zeros(diff.shape, jnp.float32)
        for t in range(TAPS):
            acc = jnp.where(diff == t, taps[view, axis, t], acc)
        return acc

    def rows(shape, start):
        return lax.broadcasted_iota(jnp.int32, shape, 0) + start

    def cols(shape):
        return lax.broadcasted_iota(jnp.int32, shape, 1)

    for s in range(0, ylen, 32):
        diff = cols((32, ylen)) - rows((32, ylen), s)
        for ref, d in ((yf, diff), (ya, -diff)):
            hi, lo = split(banded(d + RADIUS, 1))
            ref[s : s + 32, :] = jnp.concatenate([hi, hi], axis=1)
            ref[ylen + s : ylen + s + 32, :] = jnp.concatenate([lo, jnp.zeros_like(lo)], axis=1)

    def chunk(i, carry):
        s = pl.multiple_of(i * 32, 32)
        for o in range(0, full, LANES):
            shape = (32, LANES)
            diff = position(rows(shape, s), width) - position(cols(shape) + o, width)
            if o < width:
                hi, lo = split(banded(diff + RADIUS, 0))
                xfh[pl.ds(s, 32), o : o + LANES] = hi
                xfl[pl.ds(s, 32), o : o + LANES] = lo
            hi, lo = split(banded(RADIUS - diff, 0))
            xah[pl.ds(s, 32), o : o + LANES] = hi
            xal[pl.ds(s, 32), o : o + LANES] = lo
        return carry

    lax.fori_loop(0, full // 32, chunk, 0)


def z_pass(view, flipped, taps, low, own, high, out):
    depth, ylen, width = own.shape
    tiles = width // LANES
    t_of = [taps[view, 2, TAPS - 1 - t if flipped else t] for t in range(TAPS)]

    def body(i, carry):
        y = pl.ds(pl.multiple_of((i // tiles) * 8, 8), 8)
        x = pl.ds(pl.multiple_of((i % tiles) * LANES, LANES), LANES)
        acc = [None] * depth
        for p in range(depth + 2 * RADIUS):
            if p < RADIUS:
                plane = low[p, y, x]
            elif p < RADIUS + depth:
                plane = own[p - RADIUS, y, x]
            else:
                plane = high[p - RADIUS - depth, y, x]
            for o in range(depth):
                if 0 <= p - o < TAPS:
                    term = t_of[p - o] * plane
                    acc[o] = term if acc[o] is None else acc[o] + term
        for o in range(depth):
            out[o, y, x] = acc[o]
        return carry

    lax.fori_loop(0, (ylen // 8) * tiles, body, 0)


def y_pass(mat, plane):
    ylen = plane.shape[0]
    hi, lo = split(plane)
    both = dot(mat, jnp.concatenate([hi, lo], axis=0))
    return both[:ylen] + both[ylen:]


def x_pass(hi, lo, mat_hi, mat_lo):
    return dot(hi, mat_hi) + (dot(lo, mat_hi) + dot(hi, mat_lo))


def forward_kernel(view, divide, taps, low, own, high, yf, xfh, xfl, *refs):
    data = refs[0] if divide else None
    ratio, zed, hi_s, lo_s = refs[-4:]
    depth, ylen, _ = own.shape
    z_pass(view, False, taps, low, own, high, zed)
    mat = yf[...]
    for p in range(depth):
        hi, lo = split(y_pass(mat, zed[p]))
        hi_s[p * ylen : (p + 1) * ylen, :] = hi
        lo_s[p * ylen : (p + 1) * ylen, :] = lo
    for p in range(0, depth, 4):
        r = slice(p * ylen, (p + 4) * ylen)
        blurred = x_pass(hi_s[r, :], lo_s[r, :], xfh[...], xfl[...])
        blurred = blurred.reshape(4, ylen, -1)
        ratio[p : p + 4] = data[p : p + 4] / blurred if divide else blurred


def adjoint_zy_kernel(view, taps, low, own, high, ya, out, to_left, to_right, zed):
    depth, ylen, width = own.shape
    z_pass(view, True, taps, low, own, high, zed)
    mat = ya[...]
    for p in range(depth):
        out[p] = y_pass(mat, zed[p])
    lane = lax.broadcasted_iota(jnp.int32, (ylen, LANES), 1)
    half = depth // 2
    for p in range(half):
        first, first_b = out[p, :, :LANES], out[p + half, :, :LANES]
        last, last_b = out[p, :, width - LANES :], out[p + half, :, width - LANES :]
        to_left[p] = jnp.where(lane < HALF, first, pltpu.roll(first_b, HALF, 1))
        to_right[p] = jnp.where(lane < HALF, pltpu.roll(last_b, HALF, 1), last)


def adjoint_x_kernel(first, final, views, *refs):
    refs = list(refs)
    total = None if first else refs.pop(0)
    estimate = refs.pop(0) if final else None
    own, from_left, from_right, xah, xal, out, hi_s, lo_s = refs
    depth, ylen, width = own.shape
    cols = out.shape[2]
    half = depth // 2
    lane = lax.broadcasted_iota(jnp.int32, (ylen, LANES), 1)
    for p in range(depth):
        r = slice(p * ylen, (p + 1) * ylen)
        hi_s[r, :width], lo_s[r, :width] = split(own[p])
        q = p % half
        if p < half:
            halo = jnp.where(lane < HALF, from_right[q], from_left[q])
        else:
            halo = pltpu.roll(jnp.where(lane < HALF, from_left[q], from_right[q]), HALF, 1)
        hi_s[r, width:], lo_s[r, width:] = split(halo)
    for p in range(0, depth, 4):
        r = slice(p * ylen, (p + 4) * ylen)
        back = x_pass(hi_s[r, :], lo_s[r, :], xah[:, :cols], xal[:, :cols])
        logs = jnp.log(back.reshape(4, ylen, cols))
        if not first:
            logs = total[p : p + 4, :, :cols] + logs
        if final:
            logs = estimate[p : p + 4, :, :cols] * jnp.exp(logs / views)
        out[p : p + 4] = logs


def call(kernel, outs, ins, scratch, flops, moved):
    vmem = pl.BlockSpec(memory_space=pltpu.VMEM)
    return pl.pallas_call(
        kernel,
        out_shape=outs,
        in_specs=[spec if spec is not None else vmem for spec, _ in ins],
        out_specs=jax.tree.map(lambda _: vmem, outs),
        scratch_shapes=scratch,
        compiler_params=pltpu.CompilerParams(vmem_limit_bytes=VMEM_LIMIT),
        cost_estimate=pl.CostEstimate(flops=flops, bytes_accessed=moved, transcendentals=0),
    )(*[value for _, value in ins])


def per_device(views_data, estimate, kernels):
    f32, bf16 = jnp.float32, jnp.bfloat16
    depth, ylen, xlen = estimate.shape
    count = lax.axis_size("view")
    slabs = lax.axis_size("gz")
    width = xlen // count
    full = width + LANES
    me = lax.axis_index("view")
    place = ungray(me)

    def swap(value, k):
        if k == 0:
            return value
        return lax.ppermute(value, "view", [(d, d ^ k) for d in range(count)])

    up = [(i, i + 1) for i in range(slabs - 1)]
    down = [(i + 1, i) for i in range(slabs - 1)]
    rightward = [(gray(p), gray(p + 1)) for p in range(count - 1)]
    leftward = [(gray(p + 1), gray(p)) for p in range(count - 1)]

    def z_halo(value):
        low = lax.ppermute(value[depth - RADIUS :], "gz", up)
        high = lax.ppermute(value[:RADIUS], "gz", down)
        return low, high

    def columns(value, start, size):
        return lax.dynamic_slice_in_dim(value, start, size, axis=2)

    padded = jnp.pad(estimate, ((0, 0), (0, 0), (LANES, LANES)))
    own = columns(padded, place * width + LANES, width)
    right = columns(padded, place * width + LANES + width, LANES)[:, :, :HALF]
    left = columns(padded, place * width, LANES)[:, :, HALF:]
    est = jnp.concatenate([own, right, left], axis=2)
    halo = z_halo(est)
    slab_data, *halo = lax.optimization_barrier((views_data[0], *halo))

    norm = kernels[0] / jnp.sum(kernels[0], axis=-1, keepdims=True)

    def in_order(parts):
        return [lax.dynamic_index_in_dim(parts, me ^ v, 0, keepdims=False) for v in range(count)]

    taps = jnp.stack(in_order(jnp.stack([swap(norm, k) for k in range(count)])))
    data = [swap(columns(slab_data, ungray(me ^ k) * width, width), k) for k in range(count)]
    data = in_order(jnp.stack(data))

    smem = pl.BlockSpec(memory_space=pltpu.SMEM)
    shapes = [(2 * ylen, 2 * ylen)] * 2 + [(full, width)] * 2 + [(full, full)] * 2
    mats = call(
        functools.partial(matrices_kernel, width),
        [jax.ShapeDtypeStruct(s, bf16) for _ in range(count) for s in shapes],
        [(smem, taps)],
        [],
        1000000,
        1000000,
    )
    yf, ya, xfh, xfl, xah, xal = [mats[i::6] for i in range(6)]

    slab = jax.ShapeDtypeStruct((depth, ylen, width), f32)
    wide = jax.ShapeDtypeStruct((depth, ylen, full), f32)
    edge = jax.ShapeDtypeStruct((depth // 2, ylen, LANES), f32)
    rows = depth * ylen
    halves = [pltpu.VMEM((rows, full), bf16)] * 2
    work = 2 * rows * full

    for number in range(ITERS):
        last = number == ITERS - 1
        ratios, halos = [], []
        for k in range(count):
            divide = number > 0
            ratio = call(
                functools.partial(forward_kernel, k, divide),
                slab,
                [(smem, taps), (None, halo[0]), (None, est), (None, halo[1])]
                + [(None, m[k]) for m in (yf, xfh, xfl)]
                + ([(None, data[k])] if divide else []),
                [pltpu.VMEM((depth, ylen, full), f32)] + halves,
                work * 3000,
                rows * full * 16,
            )
            if not divide:
                ratio = data[k] / ratio
            ratios.append(ratio)
            halos.append(z_halo(ratio))
        total = None
        for k in range(count):
            low, high = halos[k]
            back, to_left, to_right = call(
                functools.partial(adjoint_zy_kernel, k),
                [slab, edge, edge],
                [(smem, taps), (None, low), (None, ratios[k]), (None, high), (None, ya[k])],
                [pltpu.VMEM((depth, ylen, width), f32)],
                work * 2000,
                rows * full * 16,
            )
            from_right = lax.ppermute(to_left, "view", leftward)
            from_left = lax.ppermute(to_right, "view", rightward)
            final = k == count - 1
            ins = [] if total is None else [(None, total)]
            ins += [(None, est)] if final else []
            ins += [(None, back), (None, from_left), (None, from_right)]
            ins += [(None, m[k]) for m in (xah, xal)]
            total = call(
                functools.partial(adjoint_x_kernel, total is None, final, count),
                slab if last else wide,
                ins,
                halves,
                work * 2000,
                rows * full * 16,
            )
        est = total
        if not last:
            halo = z_halo(est)

    blocks = lax.all_gather(est, "view")
    return jnp.concatenate([blocks[gray(p)] for p in range(count)], axis=2)


def solution(mesh):
    return jax.shard_map(
        per_device,
        mesh=mesh,
        in_specs=(P("view", "gz", None, None), P("gz", None, None), P("view", None, None)),
        out_specs=P("gz", None, None),
        check_vma=False,
    )
```
